128 devices in a mesh: rep: 4 (over z_hi, core), fsdp: 32 (over y, x, z_lo).
Axes of the slice: x: 4, y: 4, z: 4 (z_hi: 2, z_lo: 2; z = z_hi * 2 + z_lo), core: 2. Of those that a mesh axis runs over, the one named last changes fastest.
Arguments:
- gradient: bfloat16 [25, 1024, 5120], P(None, ('rep', 'fsdp'))
- left_basis: bfloat16 [128, 1024, 1024], P(('rep', 'fsdp')), may hold values from -0.1875 to 0.1875
- right_basis: bfloat16 [128, 1024, 1024], P(('rep', 'fsdp')), may hold values from -0.1875 to 0.1875
- moment: bfloat16 [128, 1024, 1024], P(('rep', 'fsdp')), may hold values from -0.59765625 to 0.59765625
- second: float32 [128, 1024, 1024], P(('rep', 'fsdp')), may hold values from 0.01 to 1
- owners: int32 [128], replicated, may hold values from 0 to 125, as said below
Outputs:
- direction: bfloat16 [25, 1024, 5120], P(None, ('rep', 'fsdp'))
- new_moment: bfloat16 [128, 1024, 1024], P(('rep', 'fsdp'))
- new_second: float32 [128, 1024, 1024], P(('rep', 'fsdp'))
The draws below stay inside these ranges and needn't reach their ends.
Inputs may be any that keep to these rules, and one draw needn't show every extreme that they name: `owners`: every block number 0 to 124 appears exactly once; the other 3 entries equal 125.
All inputs are finite; a program needn't handle non-finite values.
Results may differ from the reference program's by a relative error of at most 0.006.
Values may be sent and summed in bfloat16 or wider, within the bound.
No kernel may reach another device: no remote copies, remote signals or barrier semaphores. Data moves between devices by JAX's collectives and lax.ppermute only.
A program may use at most 128 MiB of HBM per device.

```python
import math
import jax
import jax.numpy as jnp
from jax import lax

D = 5120
KVW = 1024
STEP = 10
SLOTS = 128
CBLK = 5
MATS = 25
NBLK = 125
N_REP = 4
N_FSDP = 32


def block_scales(key):
    order_key = jax.random.fold_in(key, 5)
    ranks = jax.random.permutation(order_key, NBLK).astype(jnp.float32)
    levels = jnp.exp(math.log(10.0) * ranks / max(NBLK - 1, 1))
    levels = levels.reshape(MATS, 1, CBLK, 1)
    return jnp.broadcast_to(levels, (MATS, 1, CBLK, KVW)).reshape(MATS, 1, D)


def draw_gradient(key, part):
    key = jax.random.fold_in(key, 11)
    row_pos = jnp.arange(KVW, dtype=jnp.float32) / (KVW - 1)
    row_scale = jnp.exp(math.log(3.0) * row_pos)[None, :, None]
    base_vals = jax.random.normal(key, (MATS, KVW, D), jnp.float32)
    base_vals = jnp.clip(base_vals, -4.5, 4.5)
    spread = block_scales(key)
    return (base_vals * row_scale * spread).astype(jnp.bfloat16)


def draw_owners(key, part):
    key = jax.random.fold_in(key, 7)
    shuffled = jax.random.permutation(key, N_REP * N_FSDP)
    return jnp.minimum(shuffled, MATS * (D // KVW)).astype(jnp.int32)


def steps_of(stream_key, shape, shards, low, top_value):
    loudness = 1.0
    for dim, shards_of in shards:
        heights = jax.random.uniform(jax.random.fold_in(jax.random.fold_in(stream_key, 6), dim), (shards_of,), jnp.float32, low / len(shards), top_value / len(shards))
        loudness = loudness * jnp.repeat(jnp.exp(heights), shape[dim] // shards_of).reshape((-1,) + (1,) * (len(shape) - 1 - dim))
    return loudness


def centred(own_key, shape, width, reach, cuts=(), kind=jnp.bfloat16):
    drawn = jax.random.normal(own_key, shape, jnp.float32) * width
    if len(cuts) > 0:
        drawn = steps_of(own_key, shape, cuts, -0.22, 0.18) * drawn
    return jnp.clip(drawn, min=-reach, max=reach).astype(kind)


def setup_inputs(seed: int = 0) -> dict:
    splits = jax.random.split(jax.random.key(seed), 7)
    gradient = draw_gradient(jax.random.fold_in(splits[6], 71), 0)
    left_basis = centred(splits[1], (SLOTS, KVW, KVW), KVW ** -0.5, 0.1875, ((0, 128),))
    right_basis = centred(splits[2], (SLOTS, KVW, KVW), KVW ** -0.5, 0.1875, ((0, 128),))
    moment = centred(splits[3], (SLOTS, KVW, KVW), 0.1, 0.59765625, ((0, 128),))
    second = jnp.clip(jnp.exp(math.log(1.0) - 4.6051702 * jax.random.uniform(splits[4], (SLOTS, KVW, KVW), jnp.float32) ** steps_of(splits[4], (SLOTS, KVW, KVW), ((0, 128),), -0.2, 0.2)), 0.01, 1.0)
    owners = draw_owners(jax.random.fold_in(splits[6], 71), 0)
    return {"gradient": gradient, "left_basis": left_basis, "right_basis": right_basis, "moment": moment, "second": second, "owners": owners}


decay_rate = 0.95
clip_rms = 0.5
epsilon_adam = 1e-08

def reference(gradient, left_basis, right_basis, moment, second, owners):
    grad_wide = gradient.astype(jnp.float32)
    total_sq = jnp.sum(grad_wide * grad_wide)
    clip_factor = jnp.minimum(1.0, clip_rms / jnp.sqrt(total_sq / (MATS * KVW * D) + 1e-06))
    pieces = gradient.reshape(MATS, KVW, CBLK, KVW).transpose(0, 2, 1, 3).reshape(NBLK, KVW, KVW)
    padded = jnp.concatenate([pieces, jnp.zeros((1, KVW, KVW), jnp.bfloat16)], 0)
    correction = 1.0 - decay_rate ** STEP

    def one_slot(slot_id):
        block_grad = padded[owners[slot_id]]
        left_mat = left_basis[slot_id]
        right_mat = right_basis[slot_id]
        half_turn = jnp.dot(block_grad, right_mat, preferred_element_type=jnp.float32).astype(jnp.bfloat16)
        rotated = clip_factor * jnp.dot(left_mat.T, half_turn, preferred_element_type=jnp.float32)
        first_mean = decay_rate * moment[slot_id].astype(jnp.float32) + (1.0 - decay_rate) * rotated
        new_second = decay_rate * second[slot_id] + (1.0 - decay_rate) * rotated * rotated
        adam_ratio = (first_mean / correction / (jnp.sqrt(new_second / correction) + epsilon_adam)).astype(jnp.bfloat16)
        back_turn = jnp.dot(left_mat, adam_ratio, preferred_element_type=jnp.float32).astype(jnp.bfloat16)
        update = jnp.dot(back_turn, right_mat.T, preferred_element_type=jnp.float32).astype(jnp.bfloat16)
        return (first_mean.astype(jnp.bfloat16), new_second, update)
    new_moment, new_second, updates = lax.map(one_slot, jnp.arange(SLOTS, dtype=jnp.int32))
    slot_of = jnp.zeros((NBLK + 1,), jnp.int32).at[owners].set(jnp.arange(SLOTS, dtype=jnp.int32))
    placed = jnp.take(updates, slot_of[:NBLK], axis=0)
    direction = placed.reshape(MATS, CBLK, KVW, KVW).transpose(0, 2, 1, 3).reshape(MATS, KVW, D)
    return (direction, new_moment, new_second)
```

```python
import jax
import jax.numpy as jnp
from jax import lax
from jax.experimental import pallas as pl
from jax.experimental.pallas import tpu as pltpu
from jax.sharding import PartitionSpec as P

STEP = 10

decay_rate = 0.95
clip_rms = 0.5
epsilon_adam = 1e-08

AXES = ("rep", "fsdp")
TILE = 512
LANES = 128
MIB = 1024 * 1024


def block_place(block, col_blocks, width):
    mat = (block * (1024 // col_blocks + 1)) >> 10
    col = pl.multiple_of((block - mat * col_blocks) * width, width)
    return mat, col


def gather_kernel(owners_hbm, grad_ref, out_ref, owners_ref, sems):
    mats, rows, cols = grad_ref.shape
    slots = out_ref.shape[0]
    width = out_ref.shape[2] - LANES
    col_blocks = cols // width
    blocks = mats * col_blocks
    groups = sems.shape[0]
    count = slots // groups

    pltpu.sync_copy(owners_hbm, owners_ref)

    def fetch(k):
        def one(i, carry):
            s = k * count + i
            mat, col = block_place(jnp.minimum(owners_ref[s], blocks - 1), col_blocks, width)
            pltpu.make_async_copy(
                grad_ref.at[mat, :, pl.ds(col, width)], out_ref.at[s, :, pl.ds(0, width)], sems.at[k]
            ).start()
            return carry

        lax.fori_loop(0, count, one, 0, unroll=8)

    def add(s, acc):
        x = out_ref[s, :, :width].astype(jnp.float32)
        x = x * x
        parts = [x[:, c * LANES : (c + 1) * LANES] for c in range(width // LANES)]
        while len(parts) > 1:
            parts = [p + q for p, q in zip(parts[::2], parts[1::2])]
        return acc + jnp.where(owners_ref[s] < blocks, parts[0], 0.0)

    for k in range(groups):
        fetch(k)
    acc = jnp.zeros((rows, LANES), jnp.float32)
    for k in range(groups):
        part = out_ref.at[pl.ds(k * count, count), :, pl.ds(0, width)]
        pltpu.make_async_copy(part, part, sems.at[k]).wait()
        acc = lax.fori_loop(k * count, (k + 1) * count, add, acc, unroll=4)

    total = jnp.broadcast_to(jnp.sum(acc, axis=0, keepdims=True), (rows, LANES))
    high = total.astype(jnp.bfloat16).astype(jnp.float32)
    rest = jnp.where(high == jnp.inf, 0.0, total - high)
    middle = rest.astype(jnp.bfloat16).astype(jnp.float32)
    low = rest - middle
    row = lax.broadcasted_iota(jnp.int32, (rows, LANES), 0)
    note = jnp.where(row == 0, high, jnp.where(row == 1, middle, jnp.where(row == 2, low, 0.0)))
    out_ref[:, :, width:] = jnp.broadcast_to(note.astype(jnp.bfloat16)[None], (slots, rows, LANES))


def gather(owners, gradient, slots, width):
    rows = gradient.shape[1]
    return pl.pallas_call(
        gather_kernel,
        out_shape=pltpu.VMEM((slots, rows, width + LANES), jnp.bfloat16),
        in_specs=[pl.BlockSpec(memory_space=pltpu.HBM)] * 2,
        out_specs=pl.BlockSpec(memory_space=pltpu.VMEM),
        scratch_shapes=[pltpu.SMEM(owners.shape, owners.dtype), pltpu.SemaphoreType.DMA((4,))],
        compiler_params=pltpu.CompilerParams(vmem_limit_bytes=16 * MIB),
        name="gather_blocks",
    )(owners, gradient)


def place_kernel(owners_hbm, rows_ref, out_ref, owners_ref, sem):
    slots, _, width = rows_ref.shape
    mats, _, cols = out_ref.shape
    col_blocks = cols // width
    blocks = mats * col_blocks

    pltpu.sync_copy(owners_hbm, owners_ref)

    def put(s, carry):
        owner = owners_ref[s]

        @pl.when(owner < blocks)
        def _():
            mat, col = block_place(owner, col_blocks, width)
            pltpu.make_async_copy(rows_ref.at[s], out_ref.at[mat, :, pl.ds(col, width)], sem).start()

        return carry

    lax.fori_loop(0, slots, put, 0, unroll=8)
    pltpu.make_async_copy(out_ref, out_ref, sem).wait()


def place(owners, rows, out_shape):
    return pl.pallas_call(
        place_kernel,
        out_shape=jax.ShapeDtypeStruct(out_shape, jnp.bfloat16),
        in_specs=[pl.BlockSpec(memory_space=pltpu.HBM), pl.BlockSpec(memory_space=pltpu.VMEM)],
        out_specs=pl.BlockSpec(memory_space=pltpu.HBM),
        scratch_shapes=[pltpu.SMEM(owners.shape, owners.dtype), pltpu.SemaphoreType.DMA],
        compiler_params=pltpu.CompilerParams(vmem_limit_bytes=16 * MIB),
        name="place_blocks",
    )(owners, rows)


def dot(a, b):
    return jnp.dot(a, b, preferred_element_type=jnp.float32)


def step_kernel(
    elements, blocks, owners_hbm, g, r, m, s, l, u, nm_hbm, ns_hbm,
    owners_ref, lt, half, ratio, back, nm, ns, owners_sem, nm_sems, ns_sems,
):
    size = lt.shape[0]
    tiles = size // TILE

    def cols(j):
        return pl.ds(j * TILE, TILE)

    def tile_out(src, dst, sems, j):
        return pltpu.make_async_copy(src.at[:, cols(j)], dst.at[0, :, cols(j)], sems.at[j])

    owners = pltpu.make_async_copy(owners_hbm, owners_ref, owners_sem)
    owners.start()

    total_sq = jnp.sum(g[:, size:].astype(jnp.float32))
    clip_factor = jnp.minimum(1.0, clip_rms * lax.rsqrt(jnp.full((8, LANES), total_sq / elements + 1e-06, jnp.float32)))
    clip_factor = clip_factor[0:1, 0:1]
    correction = 1.0 - decay_rate**STEP

    for j in range(tiles):
        lt[:, cols(j)] = l[0, cols(j), :].T
    for j in range(tiles):
        half[:, cols(j)] = dot(g[:, :size], r[0, :, cols(j)]).astype(jnp.bfloat16)

    owners.wait()

    @pl.when(owners_ref[lax.axis_index(AXES)] >= blocks)
    def _():
        half[...] = jnp.zeros_like(half)

    for j in range(tiles):
        rotated = clip_factor * dot(lt[...], half[:, cols(j)])
        scaled = (1.0 - decay_rate) * rotated
        first_mean = decay_rate * m[0, :, cols(j)].astype(jnp.float32) + scaled
        new_second = decay_rate * s[0, :, cols(j)] + scaled * rotated
        nm[:, cols(j)] = first_mean.astype(jnp.bfloat16)
        ns[:, cols(j)] = new_second
        root = new_second * lax.rsqrt(new_second)
        denominator = root + epsilon_adam * correction**0.5
        ratio[:, cols(j)] = (first_mean * correction**-0.5 / denominator).astype(jnp.bfloat16)
    for j in range(tiles):
        tile_out(nm, nm_hbm, nm_sems, j).start()
        tile_out(ns, ns_hbm, ns_sems, j).start()
    for j in range(tiles):
        back[:, cols(j)] = dot(l[0], ratio[:, cols(j)]).astype(jnp.bfloat16)
    for j in range(tiles):
        u[:, cols(j)] = lax.dot_general(
            back[...], r[0, cols(j), :], (((1,), (1,)), ((), ())), preferred_element_type=jnp.float32
        ).astype(jnp.bfloat16)
    for j in range(tiles):
        tile_out(nm, nm_hbm, nm_sems, j).wait()
        tile_out(ns, ns_hbm, ns_sems, j).wait()


def slot_step(elements, blocks, owners, g, right, moment, second, left):
    size = g.shape[0]
    tiles = size // TILE
    low = pltpu.VMEM((size, size), jnp.bfloat16)
    wide = pltpu.VMEM((size, size), jnp.float32)
    vmem = pl.BlockSpec(memory_space=pltpu.VMEM)
    hbm = pl.BlockSpec(memory_space=pltpu.HBM)

    def kernel(*refs):
        step_kernel(elements, blocks, *refs)

    return pl.pallas_call(
        kernel,
        out_shape=(
            pltpu.VMEM((size, size), jnp.bfloat16),
            jax.ShapeDtypeStruct((1, size, size), jnp.bfloat16),
            jax.ShapeDtypeStruct((1, size, size), jnp.float32),
        ),
        in_specs=[hbm] + [vmem] * 5,
        out_specs=(vmem, hbm, hbm),
        scratch_shapes=[pltpu.SMEM(owners.shape, owners.dtype), low, low, low, low, low, wide]
        + [pltpu.SemaphoreType.DMA]
        + [pltpu.SemaphoreType.DMA((tiles,))] * 2,
        compiler_params=pltpu.CompilerParams(vmem_limit_bytes=36 * MIB),
        cost_estimate=pl.CostEstimate(flops=8 * size**3, bytes_accessed=24 * size**2, transcendentals=2 * size**2),
        name="slot_step",
    )(owners, g, right, moment, second, left)


def exchange(x):
    return lax.all_to_all(x, AXES, split_axis=0, concat_axis=0, tiled=True)


def shards(gradient, left_basis, right_basis, moment, second, owners):
    group_size = lax.axis_size(AXES)
    matrices, row_count, col_count = gradient.shape
    block_size = left_basis.shape[1]
    block_total = matrices * (col_count // block_size)
    element_count = matrices * row_count * col_count * group_size
    owners = pltpu.with_memory_space_constraint(owners, pltpu.HBM)
    gradient = pltpu.with_memory_space_constraint(gradient, pltpu.HBM)

    arrived = exchange(gather(owners, gradient, group_size, block_size))
    update, new_moment, new_second = slot_step(
        element_count, block_total, owners, arrived.reshape(block_size, block_size + LANES),
        right_basis, moment, second, left_basis,
    )
    returned = exchange(update.reshape(group_size, row_count, block_size))
    direction = place(owners, returned, gradient.shape)
    return (direction, new_moment, new_second)


def solution(mesh):
    return jax.shard_map(
        shards,
        mesh=mesh,
        in_specs=(
            P(None, AXES, None),
            P(AXES, None, None),
            P(AXES, None, None),
            P(AXES, None, None),
            P(AXES, None, None),
            P(),
        ),
        out_specs=(
            P(None, AXES, None),
            P(AXES, None, None),
            P(AXES, None, None),
        ),
        check_vma=False,
    )
```

```python
import jax
import jax.numpy as jnp
from jax import lax
from jax.experimental import pallas as pl
from jax.experimental.pallas import tpu as pltpu
from jax.sharding import PartitionSpec as P

STEP = 10

decay_rate = 0.95
clip_rms = 0.5
epsilon_adam = 1e-08

AXES = ("rep", "fsdp")
TILE = 512
LANES = 128
MIB = 1024 * 1024


def block_place(block, col_blocks, width):
    mat = (block * (1024 // col_blocks + 1)) >> 10
    col = pl.multiple_of((block - mat * col_blocks) * width, width)
    return mat, col


def gather_kernel(owners_hbm, grad_ref, out_ref, owners_ref, sems):
    mats, rows, cols = grad_ref.shape
    slots = out_ref.shape[0]
    width = out_ref.shape[2] - LANES
    col_blocks = cols // width
    blocks = mats * col_blocks
    groups = sems.shape[0]
    count = slots // groups

    pltpu.sync_copy(owners_hbm, owners_ref)

    def fetch(k):
        def one(i, carry):
            s = k * count + i
            mat, col = block_place(jnp.minimum(owners_ref[s], blocks - 1), col_blocks, width)
            pltpu.make_async_copy(
                grad_ref.at[mat, :, pl.ds(col, width)], out_ref.at[s, :, pl.ds(0, width)], sems.at[k]
            ).start()
            return carry

        lax.fori_loop(0, count, one, 0, unroll=8)

    def add(s, acc):
        x = out_ref[s, :, :width].astype(jnp.float32)
        x = x * x
        parts = [x[:, c * LANES : (c + 1) * LANES] for c in range(width // LANES)]
        while len(parts) > 1:
            parts = [p + q for p, q in zip(parts[::2], parts[1::2])]
        return acc + jnp.where(owners_ref[s] < blocks, parts[0], 0.0)

    for k in range(groups):
        fetch(k)
    acc = jnp.zeros((rows, LANES), jnp.float32)
    for k in range(groups):
        part = out_ref.at[pl.ds(k * count, count), :, pl.ds(0, width)]
        pltpu.make_async_copy(part, part, sems.at[k]).wait()
        acc = lax.fori_loop(k * count, (k + 1) * count, add, acc, unroll=4)

    total = jnp.broadcast_to(jnp.sum(acc, axis=0, keepdims=True), (rows, LANES))
    high = total.astype(jnp.bfloat16).astype(jnp.float32)
    rest = jnp.where(high == jnp.inf, 0.0, total - high)
    middle = rest.astype(jnp.bfloat16).astype(jnp.float32)
    low = rest - middle
    row = lax.broadcasted_iota(jnp.int32, (rows, LANES), 0)
    note = jnp.where(row == 0, high, jnp.where(row == 1, middle, jnp.where(row == 2, low, 0.0)))
    out_ref[:, :, width:] = jnp.broadcast_to(note.astype(jnp.bfloat16)[None], (slots, rows, LANES))


def gather(owners, gradient, slots, width):
    rows = gradient.shape[1]
    return pl.pallas_call(
        gather_kernel,
        out_shape=pltpu.VMEM((slots, rows, width + LANES), jnp.bfloat16),
        in_specs=[pl.BlockSpec(memory_space=pltpu.HBM)] * 2,
        out_specs=pl.BlockSpec(memory_space=pltpu.VMEM),
        scratch_shapes=[pltpu.SMEM(owners.shape, owners.dtype), pltpu.SemaphoreType.DMA((4,))],
        compiler_params=pltpu.CompilerParams(vmem_limit_bytes=16 * MIB),
        name="gather_blocks",
    )(owners, gradient)


def place_kernel(owners_hbm, rows_ref, out_ref, owners_ref, sem):
    slots, _, width = rows_ref.shape
    mats, _, cols = out_ref.shape
    col_blocks = cols // width
    blocks = mats * col_blocks

    pltpu.sync_copy(owners_hbm, owners_ref)

    def put(s, carry):
        owner = owners_ref[s]

        @pl.when(owner < blocks)
        def _():
            mat, col = block_place(owner, col_blocks, width)
            pltpu.make_async_copy(rows_ref.at[s], out_ref.at[mat, :, pl.ds(col, width)], sem).start()

        return carry

    lax.fori_loop(0, slots, put, 0, unroll=8)
    pltpu.make_async_copy(out_ref, out_ref, sem).wait()


def place(owners, rows, out_shape):
    return pl.pallas_call(
        place_kernel,
        out_shape=jax.ShapeDtypeStruct(out_shape, jnp.bfloat16),
        in_specs=[pl.BlockSpec(memory_space=pltpu.HBM), pl.BlockSpec(memory_space=pltpu.VMEM)],
        out_specs=pl.BlockSpec(memory_space=pltpu.HBM),
        scratch_shapes=[pltpu.SMEM(owners.shape, owners.dtype), pltpu.SemaphoreType.DMA],
        compiler_params=pltpu.CompilerParams(vmem_limit_bytes=16 * MIB),
        name="place_blocks",
    )(owners, rows)


def dot(a, b):
    return jnp.dot(a, b, preferred_element_type=jnp.float32)


def step_kernel(
    elements, blocks, owners_hbm, g, r, m, s, l_hbm, u, nm_hbm, ns_hbm,
    owners_ref, l, l_sem, lt, half, ratio, back, nm, ns, owners_sem, nm_sems, ns_sems,
):
    size = lt.shape[0]
    tiles = size // TILE

    def cols(j):
        return pl.ds(j * TILE, TILE)

    def tile_out(src, dst, sems, j):
        return pltpu.make_async_copy(src.at[:, cols(j)], dst.at[0, :, cols(j)], sems.at[j])

    owners = pltpu.make_async_copy(owners_hbm, owners_ref, owners_sem)
    owners.start()
    bring = pltpu.make_async_copy(l_hbm.at[0], l, l_sem)
    bring.start()

    total_sq = jnp.sum(g[:, size:].astype(jnp.float32))
    clip_factor = jnp.minimum(1.0, clip_rms * lax.rsqrt(jnp.full((8, LANES), total_sq / elements + 1e-06, jnp.float32)))
    clip_factor = clip_factor[0:1, 0:1]
    correction = 1.0 - decay_rate**STEP

    for j in range(tiles):
        half[:, cols(j)] = dot(g[:, :size], r[0, :, cols(j)]).astype(jnp.bfloat16)
        if j == 0:
            owners.wait()
            bring.wait()
    for j in range(tiles):
        lt[:, cols(j)] = l[cols(j), :].T
    empty = owners_ref[lax.axis_index(AXES)] >= blocks

    for j in range(tiles):
        rotated = jnp.where(empty, 0.0, clip_factor * dot(lt[...], half[:, cols(j)]))
        scaled = (1.0 - decay_rate) * rotated
        first_mean = decay_rate * m[0, :, cols(j)].astype(jnp.float32) + scaled
        new_second = decay_rate * s[0, :, cols(j)] + scaled * rotated
        nm[:, cols(j)] = first_mean.astype(jnp.bfloat16)
        ns[:, cols(j)] = new_second
        root = new_second * lax.rsqrt(new_second)
        denominator = root + epsilon_adam * correction**0.5
        ratio[:, cols(j)] = (first_mean * correction**-0.5 / denominator).astype(jnp.bfloat16)
    for j in range(tiles):
        tile_out(nm, nm_hbm, nm_sems, j).start()
        tile_out(ns, ns_hbm, ns_sems, j).start()
    for j in range(tiles):
        back[:, cols(j)] = dot(l[...], ratio[:, cols(j)]).astype(jnp.bfloat16)
    for j in range(tiles):
        u[:, cols(j)] = lax.dot_general(
            back[...], r[0, cols(j), :], (((1,), (1,)), ((), ())), preferred_element_type=jnp.float32
        ).astype(jnp.bfloat16)
    for j in range(tiles):
        tile_out(nm, nm_hbm, nm_sems, j).wait()
        tile_out(ns, ns_hbm, ns_sems, j).wait()


def slot_step(elements, blocks, owners, g, right, moment, second, left):
    size = g.shape[0]
    tiles = size // TILE
    low = pltpu.VMEM((size, size), jnp.bfloat16)
    wide = pltpu.VMEM((size, size), jnp.float32)
    vmem = pl.BlockSpec(memory_space=pltpu.VMEM)
    hbm = pl.BlockSpec(memory_space=pltpu.HBM)

    def kernel(*refs):
        step_kernel(elements, blocks, *refs)

    return pl.pallas_call(
        kernel,
        out_shape=(
            pltpu.VMEM((size, size), jnp.bfloat16),
            jax.ShapeDtypeStruct((1, size, size), jnp.bfloat16),
            jax.ShapeDtypeStruct((1, size, size), jnp.float32),
        ),
        in_specs=[hbm] + [vmem] * 4 + [hbm],
        out_specs=(vmem, hbm, hbm),
        scratch_shapes=[pltpu.SMEM(owners.shape, owners.dtype), low, pltpu.SemaphoreType.DMA, low, low, low, low, low, wide]
        + [pltpu.SemaphoreType.DMA]
        + [pltpu.SemaphoreType.DMA((tiles,))] * 2,
        compiler_params=pltpu.CompilerParams(vmem_limit_bytes=36 * MIB),
        cost_estimate=pl.CostEstimate(flops=8 * size**3, bytes_accessed=24 * size**2, transcendentals=2 * size**2),
        name="slot_step",
    )(owners, g, right, moment, second, left)


def exchange(x):
    return lax.all_to_all(x, AXES, split_axis=0, concat_axis=0, tiled=True)


def shards(gradient, left_basis, right_basis, moment, second, owners):
    group_size = lax.axis_size(AXES)
    matrices, row_count, col_count = gradient.shape
    block_size = left_basis.shape[1]
    block_total = matrices * (col_count // block_size)
    element_count = matrices * row_count * col_count * group_size
    owners = pltpu.with_memory_space_constraint(owners, pltpu.HBM)
    gradient = pltpu.with_memory_space_constraint(gradient, pltpu.HBM)

    arrived = exchange(gather(owners, gradient, group_size, block_size))
    update, new_moment, new_second = slot_step(
        element_count, block_total, owners, arrived.reshape(block_size, block_size + LANES),
        right_basis, moment, second, left_basis,
    )
    returned = exchange(update.reshape(group_size, row_count, block_size))
    direction = place(owners, returned, gradient.shape)
    return (direction, new_moment, new_second)


def solution(mesh):
    return jax.shard_map(
        shards,
        mesh=mesh,
        in_specs=(
            P(None, AXES, None),
            P(AXES, None, None),
            P(AXES, None, None),
            P(AXES, None, None),
            P(AXES, None, None),
            P(),
        ),
        out_specs=(
            P(None, AXES, None),
            P(AXES, None, None),
            P(AXES, None, None),
        ),
        check_vma=False,
    )
```

```python
import jax
import jax.numpy as jnp
from jax import lax
from jax.experimental import pallas as pl
from jax.experimental.pallas import tpu as pltpu
from jax.sharding import PartitionSpec as P

STEP = 10

decay_rate = 0.95
clip_rms = 0.5
epsilon_adam = 1e-08

AXES = ("rep", "fsdp")
TILE = 512
LANES = 128
MIB = 1024 * 1024


def block_place(block, col_blocks, width):
    mat = (block * (1024 // col_blocks + 1)) >> 10
    col = pl.multiple_of((block - mat * col_blocks) * width, width)
    return mat, col


def gather_kernel(owners_hbm, grad_hbm, out_ref, owners_ref, slot_of, grad, owners_sem, sems):
    mats, rows, cols = grad_hbm.shape
    slots = out_ref.shape[0]
    width = out_ref.shape[2] - LANES
    col_blocks = cols // width
    blocks = mats * col_blocks
    pieces = sems.shape[0]
    step = mats // pieces

    owners = pltpu.make_async_copy(owners_hbm, owners_ref, owners_sem)
    owners.start()
    loads = []
    for k in range(pieces):
        part = pl.ds(k * step, step)
        loads.append(pltpu.make_async_copy(grad_hbm.at[part], grad.at[part], sems.at[k]))
        loads[-1].start()

    owners.wait()

    def invert(s, spare):
        owner = owners_ref[s]
        slot_of[owner] = s
        shifted = (s,) + spare[:-1]
        return tuple(jnp.where(owner >= blocks, new, old) for new, old in zip(shifted, spare))

    spare = lax.fori_loop(0, slots, invert, (jnp.int32(0),) * (slots - blocks), unroll=16)
    for s in spare:
        out_ref[s, :, :width] = jnp.zeros((rows, width), jnp.bfloat16)

    def send(i, acc):
        for c in range(col_blocks):
            x = grad[i, :, c * width : (c + 1) * width]
            out_ref[slot_of[i * col_blocks + c], :, :width] = x
            x = x.astype(jnp.float32)
            x = x * x
            parts = [x[:, k * LANES : (k + 1) * LANES] for k in range(width // LANES)]
            while len(parts) > 1:
                parts = [p + q for p, q in zip(parts[::2], parts[1::2])]
            acc = acc + parts[0]
        return acc

    acc = jnp.zeros((rows, LANES), jnp.float32)
    for k in range(pieces):
        loads[k].wait()
        acc = lax.fori_loop(k * step, (k + 1) * step, send, acc)

    total = jnp.broadcast_to(jnp.sum(acc, axis=0, keepdims=True), (rows, LANES))
    high = total.astype(jnp.bfloat16).astype(jnp.float32)
    rest = jnp.where(high == jnp.inf, 0.0, total - high)
    middle = rest.astype(jnp.bfloat16).astype(jnp.float32)
    low = rest - middle
    row = lax.broadcasted_iota(jnp.int32, (rows, LANES), 0)
    note = jnp.where(row == 0, high, jnp.where(row == 1, middle, jnp.where(row == 2, low, 0.0)))
    out_ref[:, :, width:] = jnp.broadcast_to(note.astype(jnp.bfloat16)[None], (slots, rows, LANES))


def gather(owners, gradient, slots, width):
    mats, rows, _ = gradient.shape
    pieces = 5 if mats % 5 == 0 else 1
    table = pltpu.SMEM((slots,), jnp.int32)
    return pl.pallas_call(
        gather_kernel,
        out_shape=pltpu.VMEM((slots, rows, width + LANES), jnp.bfloat16),
        in_specs=[pl.BlockSpec(memory_space=pltpu.HBM)] * 2,
        out_specs=pl.BlockSpec(memory_space=pltpu.VMEM),
        scratch_shapes=[
            table,
            table,
            pltpu.VMEM(gradient.shape, jnp.bfloat16),
            pltpu.SemaphoreType.DMA,
            pltpu.SemaphoreType.DMA((pieces,)),
        ],
        compiler_params=pltpu.CompilerParams(vmem_limit_bytes=16 * MIB),
        name="gather_blocks",
    )(owners, gradient)


def place_kernel(owners_hbm, rows_ref, out_ref, owners_ref, sem):
    slots, _, width = rows_ref.shape
    mats, _, cols = out_ref.shape
    col_blocks = cols // width
    blocks = mats * col_blocks

    pltpu.sync_copy(owners_hbm, owners_ref)

    def put(s, carry):
        owner = owners_ref[s]

        @pl.when(owner < blocks)
        def _():
            mat, col = block_place(owner, col_blocks, width)
            pltpu.make_async_copy(rows_ref.at[s], out_ref.at[mat, :, pl.ds(col, width)], sem).start()

        return carry

    lax.fori_loop(0, slots, put, 0, unroll=8)
    pltpu.make_async_copy(out_ref, out_ref, sem).wait()


def place(owners, rows, out_shape):
    return pl.pallas_call(
        place_kernel,
        out_shape=jax.ShapeDtypeStruct(out_shape, jnp.bfloat16),
        in_specs=[pl.BlockSpec(memory_space=pltpu.HBM), pl.BlockSpec(memory_space=pltpu.VMEM)],
        out_specs=pl.BlockSpec(memory_space=pltpu.HBM),
        scratch_shapes=[pltpu.SMEM(owners.shape, owners.dtype), pltpu.SemaphoreType.DMA],
        compiler_params=pltpu.CompilerParams(vmem_limit_bytes=16 * MIB),
        name="place_blocks",
    )(owners, rows)


def dot(a, b):
    return jnp.dot(a, b, preferred_element_type=jnp.float32)


def step_kernel(
    elements, g, r, l, m_hbm, s, u, nm_hbm, ns_hbm,
    m, lt, half, ratio, back, nm, ns, m_sem, nm_sems, ns_sems,
):
    size = lt.shape[0]
    tiles = size // TILE

    def cols(j):
        return pl.ds(j * TILE, TILE)

    def tile_out(src, dst, sems, j):
        return pltpu.make_async_copy(src.at[:, cols(j)], dst.at[0, :, cols(j)], sems.at[j])

    loads = [
        pltpu.make_async_copy(m_hbm.at[0, pl.ds(k * size // 4, size // 4)], m.at[pl.ds(k * size // 4, size // 4)], m_sem.at[k])
        for k in range(4)
    ]
    for load in loads:
        load.start()

    total_sq = jnp.sum(g[:, size:].astype(jnp.float32))
    clip_factor = jnp.minimum(1.0, clip_rms * lax.rsqrt(jnp.full((8, LANES), total_sq / elements + 1e-06, jnp.float32)))
    clip_factor = clip_factor[0:1, 0:1]
    correction = 1.0 - decay_rate**STEP

    for j in range(tiles):
        half[:, cols(j)] = dot(g[:, :size], r[0, :, cols(j)]).astype(jnp.bfloat16)
        if j == 0:
            for load in loads:
                load.wait()
    for j in range(tiles):
        lt[:, cols(j)] = l[0, cols(j), :].T
    for j in range(tiles):
        rotated = clip_factor * dot(lt[...], half[:, cols(j)])
        scaled = (1.0 - decay_rate) * rotated
        first_mean = decay_rate * m[:, cols(j)].astype(jnp.float32) + scaled
        new_second = decay_rate * s[0, :, cols(j)] + scaled * rotated
        nm[:, cols(j)] = first_mean.astype(jnp.bfloat16)
        ns[:, cols(j)] = new_second
        root = new_second * lax.rsqrt(new_second)
        denominator = root + epsilon_adam * correction**0.5
        ratio[:, cols(j)] = (first_mean * correction**-0.5 / denominator).astype(jnp.bfloat16)
    for j in range(tiles):
        tile_out(nm, nm_hbm, nm_sems, j).start()
        tile_out(ns, ns_hbm, ns_sems, j).start()
    for j in range(tiles):
        back[:, cols(j)] = dot(l[0], ratio[:, cols(j)]).astype(jnp.bfloat16)
    for j in range(tiles):
        u[:, cols(j)] = lax.dot_general(
            back[...], r[0, cols(j), :], (((1,), (1,)), ((), ())), preferred_element_type=jnp.float32
        ).astype(jnp.bfloat16)
    for j in range(tiles):
        tile_out(nm, nm_hbm, nm_sems, j).wait()
        tile_out(ns, ns_hbm, ns_sems, j).wait()


def slot_step(elements, g, right, left, moment, second):
    size = g.shape[0]
    tiles = size // TILE
    low = pltpu.VMEM((size, size), jnp.bfloat16)
    wide = pltpu.VMEM((size, size), jnp.float32)
    vmem = pl.BlockSpec(memory_space=pltpu.VMEM)
    hbm = pl.BlockSpec(memory_space=pltpu.HBM)

    def kernel(*refs):
        step_kernel(elements, *refs)

    return pl.pallas_call(
        kernel,
        out_shape=(
            pltpu.VMEM((size, size), jnp.bfloat16),
            jax.ShapeDtypeStruct((1, size, size), jnp.bfloat16),
            jax.ShapeDtypeStruct((1, size, size), jnp.float32),
        ),
        in_specs=[vmem] * 3 + [hbm, vmem],
        out_specs=(vmem, hbm, hbm),
        scratch_shapes=[low, low, low, low, low, low, wide]
        + [pltpu.SemaphoreType.DMA((4,))]
        + [pltpu.SemaphoreType.DMA((tiles,))] * 2,
        compiler_params=pltpu.CompilerParams(vmem_limit_bytes=36 * MIB),
        cost_estimate=pl.CostEstimate(flops=8 * size**3, bytes_accessed=24 * size**2, transcendentals=2 * size**2),
        name="slot_step",
    )(g, right, left, moment, second)


def exchange(x):
    return lax.all_to_all(x, AXES, split_axis=0, concat_axis=0, tiled=True)


def shards(gradient, left_basis, right_basis, moment, second, owners):
    group_size = lax.axis_size(AXES)
    matrices, row_count, col_count = gradient.shape
    block_size = left_basis.shape[1]
    element_count = matrices * row_count * col_count * group_size
    owners = pltpu.with_memory_space_constraint(owners, pltpu.HBM)
    gradient = pltpu.with_memory_space_constraint(gradient, pltpu.HBM)
    moment = pltpu.with_memory_space_constraint(moment, pltpu.HBM)

    sending = gather(owners, gradient, group_size, block_size)
    arrived = exchange(sending)
    update, new_moment, new_second = slot_step(
        element_count, arrived.reshape(block_size, block_size + LANES),
        right_basis, left_basis, moment, second,
    )
    returned = exchange(update.reshape(group_size, row_count, block_size))
    direction = place(owners, returned, gradient.shape)
    return (direction, new_moment, new_second)


def solution(mesh):
    return jax.shard_map(
        shards,
        mesh=mesh,
        in_specs=(
            P(None, AXES, None),
            P(AXES, None, None),
            P(AXES, None, None),
            P(AXES, None, None),
            P(AXES, None, None),
            P(),
        ),
        out_specs=(
            P(None, AXES, None),
            P(AXES, None, None),
            P(AXES, None, None),
        ),
        check_vma=False,
    )
```

```python
import jax
import jax.numpy as jnp
from jax import lax
from jax.experimental import pallas as pl
from jax.experimental.pallas import tpu as pltpu
from jax.sharding import PartitionSpec as P

STEP = 10

decay_rate = 0.95
clip_rms = 0.5
epsilon_adam = 1e-08

AXES = ("rep", "fsdp")
TILE = 512
LANES = 128
MIB = 1024 * 1024


def block_place(block, col_blocks, width):
    mat = (block * (1024 // col_blocks + 1)) >> 10
    col = pl.multiple_of((block - mat * col_blocks) * width, width)
    return mat, col


def gather_kernel(owners_hbm, grad_hbm, out_ref, owners_ref, slot_of, grad, owners_sem, sems):
    mats, rows, cols = grad_hbm.shape
    slots = out_ref.shape[0]
    width = out_ref.shape[2] - LANES
    col_blocks = cols // width
    blocks = mats * col_blocks
    pieces = sems.shape[0]
    step = mats // pieces

    owners = pltpu.make_async_copy(owners_hbm, owners_ref, owners_sem)
    owners.start()
    loads = []
    for k in range(pieces):
        part = pl.ds(k * step, step)
        loads.append(pltpu.make_async_copy(grad_hbm.at[part], grad.at[part], sems.at[k]))
        loads[-1].start()

    owners.wait()

    def invert(s, spare):
        owner = owners_ref[s]
        slot_of[owner] = s
        shifted = (s,) + spare[:-1]
        return tuple(jnp.where(owner >= blocks, new, old) for new, old in zip(shifted, spare))

    spare = lax.fori_loop(0, slots, invert, (jnp.int32(0),) * (slots - blocks), unroll=16)
    for s in spare:
        out_ref[s, :, :width] = jnp.zeros((rows, width), jnp.bfloat16)

    def send(i, acc):
        for c in range(col_blocks):
            x = grad[i, :, c * width : (c + 1) * width]
            out_ref[slot_of[i * col_blocks + c], :, :width] = x
            x = x.astype(jnp.float32)
            x = x * x
            parts = [x[:, k * LANES : (k + 1) * LANES] for k in range(width // LANES)]
            while len(parts) > 1:
                parts = [p + q for p, q in zip(parts[::2], parts[1::2])]
            acc = acc + parts[0]
        return acc

    acc = jnp.zeros((rows, LANES), jnp.float32)
    for k in range(pieces):
        loads[k].wait()
        acc = lax.fori_loop(k * step, (k + 1) * step, send, acc)

    total = jnp.broadcast_to(jnp.sum(acc, axis=0, keepdims=True), (rows, LANES))
    high = total.astype(jnp.bfloat16).astype(jnp.float32)
    rest = jnp.where(high == jnp.inf, 0.0, total - high)
    middle = rest.astype(jnp.bfloat16).astype(jnp.float32)
    low = rest - middle
    row = lax.broadcasted_iota(jnp.int32, (rows, LANES), 0)
    note = jnp.where(row == 0, high, jnp.where(row == 1, middle, jnp.where(row == 2, low, 0.0)))
    out_ref[:, :, width:] = jnp.broadcast_to(note.astype(jnp.bfloat16)[None], (slots, rows, LANES))


def gather(owners, gradient, slots, width):
    mats, rows, _ = gradient.shape
    pieces = 5 if mats % 5 == 0 else 1
    table = pltpu.SMEM((slots,), jnp.int32)
    return pl.pallas_call(
        gather_kernel,
        out_shape=pltpu.VMEM((slots, rows, width + LANES), jnp.bfloat16),
        in_specs=[pl.BlockSpec(memory_space=pltpu.HBM)] * 2,
        out_specs=pl.BlockSpec(memory_space=pltpu.VMEM),
        scratch_shapes=[
            table,
            table,
            pltpu.VMEM(gradient.shape, jnp.bfloat16),
            pltpu.SemaphoreType.DMA,
            pltpu.SemaphoreType.DMA((pieces,)),
        ],
        compiler_params=pltpu.CompilerParams(vmem_limit_bytes=16 * MIB),
        name="gather_blocks",
    )(owners, gradient)


def place_kernel(owners_ref, rows_ref, out_ref, sem):
    slots, _, width = rows_ref.shape
    mats, _, cols = out_ref.shape
    col_blocks = cols // width
    blocks = mats * col_blocks

    def put(s, carry):
        owner = owners_ref[s]

        @pl.when(owner < blocks)
        def _():
            mat, col = block_place(owner, col_blocks, width)
            pltpu.make_async_copy(rows_ref.at[s], out_ref.at[mat, :, pl.ds(col, width)], sem).start()

        return carry

    lax.fori_loop(0, slots, put, 0, unroll=8)
    pltpu.make_async_copy(out_ref, out_ref, sem).wait()


def place(owners, rows, out_shape):
    return pl.pallas_call(
        place_kernel,
        out_shape=jax.ShapeDtypeStruct(out_shape, jnp.bfloat16),
        in_specs=[pl.BlockSpec(memory_space=pltpu.SMEM), pl.BlockSpec(memory_space=pltpu.VMEM)],
        out_specs=pl.BlockSpec(memory_space=pltpu.HBM),
        scratch_shapes=[pltpu.SemaphoreType.DMA],
        compiler_params=pltpu.CompilerParams(vmem_limit_bytes=16 * MIB),
        name="place_blocks",
    )(owners, rows)


def dot(a, b):
    return jnp.dot(a, b, preferred_element_type=jnp.float32)


def step_kernel(
    elements, g, r, l, m_hbm, s, u, nm_hbm, ns_hbm,
    m, lt, half, ratio, back, nm, ns, m_sem, nm_sems, ns_sems,
):
    size = lt.shape[0]
    tiles = size // TILE

    def cols(j):
        return pl.ds(j * TILE, TILE)

    def tile_out(src, dst, sems, j):
        return pltpu.make_async_copy(src.at[:, cols(j)], dst.at[0, :, cols(j)], sems.at[j])

    loads = [
        pltpu.make_async_copy(m_hbm.at[0, pl.ds(k * size // 4, size // 4)], m.at[pl.ds(k * size // 4, size // 4)], m_sem.at[k])
        for k in range(4)
    ]
    for load in loads:
        load.start()

    total_sq = jnp.sum(g[:, size:].astype(jnp.float32), axis=(0, 1), keepdims=True)
    clip_factor = jnp.minimum(1.0, clip_rms * lax.rsqrt(total_sq / elements + 1e-06))
    correction = 1.0 - decay_rate**STEP

    for j in range(tiles):
        half[:, cols(j)] = dot(g[:, :size], r[0, :, cols(j)]).astype(jnp.bfloat16)
    for load in loads:
        load.wait()
    for j in range(tiles):
        lt[:, cols(j)] = l[0, cols(j), :].T
    for j in range(tiles):
        rotated = clip_factor * dot(lt[...], half[:, cols(j)])
        scaled = (1.0 - decay_rate) * rotated
        first_mean = decay_rate * m[:, cols(j)].astype(jnp.float32) + scaled
        new_second = decay_rate * s[0, :, cols(j)] + scaled * rotated
        nm[:, cols(j)] = first_mean.astype(jnp.bfloat16)
        ns[:, cols(j)] = new_second
        root = new_second * lax.rsqrt(new_second)
        denominator = root + epsilon_adam * correction**0.5
        ratio[:, cols(j)] = (first_mean * correction**-0.5 / denominator).astype(jnp.bfloat16)
    for j in range(tiles):
        tile_out(nm, nm_hbm, nm_sems, j).start()
        tile_out(ns, ns_hbm, ns_sems, j).start()
    for j in range(tiles):
        back[:, cols(j)] = dot(l[0], ratio[:, cols(j)]).astype(jnp.bfloat16)
    for j in range(tiles):
        u[:, cols(j)] = lax.dot_general(
            back[...], r[0, cols(j), :], (((1,), (1,)), ((), ())), preferred_element_type=jnp.float32
        ).astype(jnp.bfloat16)
    for j in range(tiles):
        tile_out(nm, nm_hbm, nm_sems, j).wait()
        tile_out(ns, ns_hbm, ns_sems, j).wait()


def slot_step(elements, g, right, left, moment, second):
    size = g.shape[0]
    tiles = size // TILE
    low = pltpu.VMEM((size, size), jnp.bfloat16)
    wide = pltpu.VMEM((size, size), jnp.float32)
    vmem = pl.BlockSpec(memory_space=pltpu.VMEM)
    hbm = pl.BlockSpec(memory_space=pltpu.HBM)

    def kernel(*refs):
        step_kernel(elements, *refs)

    return pl.pallas_call(
        kernel,
        out_shape=(
            pltpu.VMEM((size, size), jnp.bfloat16),
            jax.ShapeDtypeStruct((1, size, size), jnp.bfloat16),
            jax.ShapeDtypeStruct((1, size, size), jnp.float32),
        ),
        in_specs=[vmem] * 3 + [hbm, vmem],
        out_specs=(vmem, hbm, hbm),
        scratch_shapes=[low, low, low, low, low, low, wide]
        + [pltpu.SemaphoreType.DMA((4,))]
        + [pltpu.SemaphoreType.DMA((tiles,))] * 2,
        compiler_params=pltpu.CompilerParams(vmem_limit_bytes=36 * MIB),
        cost_estimate=pl.CostEstimate(flops=8 * size**3, bytes_accessed=24 * size**2, transcendentals=2 * size**2),
        name="slot_step",
    )(g, right, left, moment, second)


def exchange(x):
    return lax.all_to_all(x, AXES, split_axis=0, concat_axis=0, tiled=True)


def shards(gradient, left_basis, right_basis, moment, second, owners):
    group_size = lax.axis_size(AXES)
    matrices, row_count, col_count = gradient.shape
    block_size = left_basis.shape[1]
    element_count = matrices * row_count * col_count * group_size
    gradient = pltpu.with_memory_space_constraint(gradient, pltpu.HBM)
    moment = pltpu.with_memory_space_constraint(moment, pltpu.HBM)

    sending = gather(pltpu.with_memory_space_constraint(owners, pltpu.HBM), gradient, group_size, block_size)
    arrived = exchange(sending)
    update, new_moment, new_second = slot_step(
        element_count, arrived.reshape(block_size, block_size + LANES),
        right_basis, left_basis, moment, second,
    )
    returned = exchange(update.reshape(group_size, row_count, block_size))
    direction = place(owners, returned, gradient.shape)
    return (direction, new_moment, new_second)


def solution(mesh):
    return jax.shard_map(
        shards,
        mesh=mesh,
        in_specs=(
            P(None, AXES, None),
            P(AXES, None, None),
            P(AXES, None, None),
            P(AXES, None, None),
            P(AXES, None, None),
            P(),
        ),
        out_specs=(
            P(None, AXES, None),
            P(AXES, None, None),
            P(AXES, None, None),
        ),
        check_vma=False,
    )
```

```python
import jax
import jax.numpy as jnp
from jax import lax
from jax.experimental import pallas as pl
from jax.experimental.pallas import tpu as pltpu
from jax.sharding import PartitionSpec as P

STEP = 10

decay_rate = 0.95
clip_rms = 0.5
epsilon_adam = 1e-08

AXES = ("rep", "fsdp")
TILE = 512
LANES = 128
MIB = 1024 * 1024


def block_place(block, col_blocks, width):
    mat = (block * (1024 // col_blocks + 1)) >> 10
    col = pl.multiple_of((block - mat * col_blocks) * width, width)
    return mat, col


def gather_kernel(owners_hbm, grad_hbm, out_ref, owners_ref, slot_of, grad, owners_sem, sems):
    mats, rows, cols = grad_hbm.shape
    slots = out_ref.shape[0]
    width = out_ref.shape[2] - LANES
    col_blocks = cols // width
    blocks = mats * col_blocks
    pieces = sems.shape[0]
    step = mats // pieces

    owners = pltpu.make_async_copy(owners_hbm, owners_ref, owners_sem)
    owners.start()
    loads = []
    for k in range(pieces):
        part = pl.ds(k * step, step)
        loads.append(pltpu.make_async_copy(grad_hbm.at[part], grad.at[part], sems.at[k]))
        loads[-1].start()

    owners.wait()

    def invert(s, spare):
        owner = owners_ref[s]
        slot_of[owner] = s
        shifted = (s,) + spare[:-1]
        return tuple(jnp.where(owner >= blocks, new, old) for new, old in zip(shifted, spare))

    spare = lax.fori_loop(0, slots, invert, (jnp.int32(0),) * (slots - blocks), unroll=16)
    for s in spare:
        out_ref[s, :, :width] = jnp.zeros((rows, width), jnp.bfloat16)

    def send(i, acc):
        for c in range(col_blocks):
            x = grad[i, :, c * width : (c + 1) * width]
            out_ref[slot_of[i * col_blocks + c], :, :width] = x
            x = x.astype(jnp.float32)
            x = x * x
            parts = [x[:, k * LANES : (k + 1) * LANES] for k in range(width // LANES)]
            while len(parts) > 1:
                parts = [p + q for p, q in zip(parts[::2], parts[1::2])]
            acc = acc + parts[0]
        return acc

    acc = jnp.zeros((rows, LANES), jnp.float32)
    for k in range(pieces):
        loads[k].wait()
        acc = lax.fori_loop(k * step, (k + 1) * step, send, acc)

    total = jnp.broadcast_to(jnp.sum(acc, axis=0, keepdims=True), (rows, LANES))
    high = total.astype(jnp.bfloat16).astype(jnp.float32)
    rest = jnp.where(high == jnp.inf, 0.0, total - high)
    middle = rest.astype(jnp.bfloat16).astype(jnp.float32)
    low = rest - middle
    row = lax.broadcasted_iota(jnp.int32, (rows, LANES), 0)
    note = jnp.where(row == 0, high, jnp.where(row == 1, middle, jnp.where(row == 2, low, 0.0)))
    out_ref[:, :, width:] = jnp.broadcast_to(note.astype(jnp.bfloat16)[None], (slots, rows, LANES))


def gather(owners, gradient, slots, width):
    mats, rows, _ = gradient.shape
    pieces = 5 if mats % 5 == 0 else 1
    table = pltpu.SMEM((slots,), jnp.int32)
    return pl.pallas_call(
        gather_kernel,
        out_shape=pltpu.VMEM((slots, rows, width + LANES), jnp.bfloat16),
        in_specs=[pl.BlockSpec(memory_space=pltpu.HBM)] * 2,
        out_specs=pl.BlockSpec(memory_space=pltpu.VMEM),
        scratch_shapes=[
            table,
            table,
            pltpu.VMEM(gradient.shape, jnp.bfloat16),
            pltpu.SemaphoreType.DMA,
            pltpu.SemaphoreType.DMA((pieces,)),
        ],
        compiler_params=pltpu.CompilerParams(vmem_limit_bytes=16 * MIB),
        cost_estimate=pl.CostEstimate(flops=10**11, bytes_accessed=10**8, transcendentals=0),
        name="gather_blocks",
    )(owners, gradient)


def place_kernel(owners_ref, rows_ref, out_ref, sem):
    slots, _, width = rows_ref.shape
    mats, _, cols = out_ref.shape
    col_blocks = cols // width
    blocks = mats * col_blocks

    def put(s, carry):
        owner = owners_ref[s]

        @pl.when(owner < blocks)
        def _():
            mat, col = block_place(owner, col_blocks, width)
            pltpu.make_async_copy(rows_ref.at[s], out_ref.at[mat, :, pl.ds(col, width)], sem).start()

        return carry

    lax.fori_loop(0, slots, put, 0, unroll=8)
    pltpu.make_async_copy(out_ref, out_ref, sem).wait()


def place(owners, rows, out_shape):
    return pl.pallas_call(
        place_kernel,
        out_shape=jax.ShapeDtypeStruct(out_shape, jnp.bfloat16),
        in_specs=[pl.BlockSpec(memory_space=pltpu.SMEM), pl.BlockSpec(memory_space=pltpu.VMEM)],
        out_specs=pl.BlockSpec(memory_space=pltpu.HBM),
        scratch_shapes=[pltpu.SemaphoreType.DMA],
        compiler_params=pltpu.CompilerParams(vmem_limit_bytes=16 * MIB),
        name="place_blocks",
    )(owners, rows)


def dot(a, b):
    return jnp.dot(a, b, preferred_element_type=jnp.float32)


def step_kernel(
    elements, g, r, l, m, s, u, nm_hbm, ns_hbm,
    lt, half, ratio, back, nm, ns, nm_sems, ns_sems,
):
    size = lt.shape[0]
    tiles = size // TILE

    def cols(j):
        return pl.ds(j * TILE, TILE)

    def tile_out(src, dst, sems, j):
        return pltpu.make_async_copy(src.at[:, cols(j)], dst.at[0, :, cols(j)], sems.at[j])

    total_sq = jnp.sum(g[:, size:].astype(jnp.float32), axis=(0, 1), keepdims=True)
    clip_factor = jnp.minimum(1.0, clip_rms * lax.rsqrt(total_sq / elements + 1e-06))
    correction = 1.0 - decay_rate**STEP

    for j in range(tiles):
        half[:, cols(j)] = dot(g[:, :size], r[0, :, cols(j)]).astype(jnp.bfloat16)
    for j in range(tiles):
        lt[:, cols(j)] = l[0, cols(j), :].T
    for j in range(tiles):
        rotated = clip_factor * dot(lt[...], half[:, cols(j)])
        scaled = (1.0 - decay_rate) * rotated
        first_mean = decay_rate * m[0, :, cols(j)].astype(jnp.float32) + scaled
        new_second = decay_rate * s[0, :, cols(j)] + scaled * rotated
        nm[:, cols(j)] = first_mean.astype(jnp.bfloat16)
        ns[:, cols(j)] = new_second
        root = new_second * lax.rsqrt(new_second)
        denominator = root + epsilon_adam * correction**0.5
        ratio[:, cols(j)] = (first_mean * correction**-0.5 / denominator).astype(jnp.bfloat16)
    for j in range(tiles):
        tile_out(nm, nm_hbm, nm_sems, j).start()
        tile_out(ns, ns_hbm, ns_sems, j).start()
    for j in range(tiles):
        back[:, cols(j)] = dot(l[0], ratio[:, cols(j)]).astype(jnp.bfloat16)
    for j in range(tiles):
        u[:, cols(j)] = lax.dot_general(
            back[...], r[0, cols(j), :], (((1,), (1,)), ((), ())), preferred_element_type=jnp.float32
        ).astype(jnp.bfloat16)
    for j in range(tiles):
        tile_out(nm, nm_hbm, nm_sems, j).wait()
        tile_out(ns, ns_hbm, ns_sems, j).wait()


def slot_step(elements, g, right, left, moment, second):
    size = g.shape[0]
    tiles = size // TILE
    low = pltpu.VMEM((size, size), jnp.bfloat16)
    wide = pltpu.VMEM((size, size), jnp.float32)
    vmem = pl.BlockSpec(memory_space=pltpu.VMEM)
    hbm = pl.BlockSpec(memory_space=pltpu.HBM)

    def kernel(*refs):
        step_kernel(elements, *refs)

    return pl.pallas_call(
        kernel,
        out_shape=(
            pltpu.VMEM((size, size), jnp.bfloat16),
            jax.ShapeDtypeStruct((1, size, size), jnp.bfloat16),
            jax.ShapeDtypeStruct((1, size, size), jnp.float32),
        ),
        in_specs=[vmem] * 5,
        out_specs=(vmem, hbm, hbm),
        scratch_shapes=[low, low, low, low, low, wide]
        + [pltpu.SemaphoreType.DMA((tiles,))] * 2,
        compiler_params=pltpu.CompilerParams(vmem_limit_bytes=36 * MIB),
        cost_estimate=pl.CostEstimate(flops=8 * size**3, bytes_accessed=24 * size**2, transcendentals=2 * size**2),
        name="slot_step",
    )(g, right, left, moment, second)


def exchange(x):
    return lax.all_to_all(x, AXES, split_axis=0, concat_axis=0, tiled=True)


def shards(gradient, left_basis, right_basis, moment, second, owners):
    group_size = lax.axis_size(AXES)
    matrices, row_count, col_count = gradient.shape
    block_size = left_basis.shape[1]
    element_count = matrices * row_count * col_count * group_size
    gradient = pltpu.with_memory_space_constraint(gradient, pltpu.HBM)

    sending = gather(pltpu.with_memory_space_constraint(owners, pltpu.HBM), gradient, group_size, block_size)
    arrived = exchange(sending)
    update, new_moment, new_second = slot_step(
        element_count, arrived.reshape(block_size, block_size + LANES),
        right_basis, left_basis, moment, second,
    )
    returned = exchange(update.reshape(group_size, row_count, block_size))
    direction = place(owners, returned, gradient.shape)
    return (direction, new_moment, new_second)


def solution(mesh):
    return jax.shard_map(
        shards,
        mesh=mesh,
        in_specs=(
            P(None, AXES, None),
            P(AXES, None, None),
            P(AXES, None, None),
            P(AXES, None, None),
            P(AXES, None, None),
            P(),
        ),
        out_specs=(
            P(None, AXES, None),
            P(AXES, None, None),
            P(AXES, None, None),
        ),
        check_vma=False,
    )
```

```python
import jax
import jax.numpy as jnp
from jax import lax
from jax.experimental import pallas as pl
from jax.experimental.pallas import tpu as pltpu
from jax.sharding import PartitionSpec as P

STEP = 10

decay_rate = 0.95
clip_rms = 0.5
epsilon_adam = 1e-08

AXES = ("rep", "fsdp")
TILE = 512
LANES = 128
MIB = 1024 * 1024


def block_place(block, col_blocks, width):
    mat = (block * (1024 // col_blocks + 1)) >> 10
    col = pl.multiple_of((block - mat * col_blocks) * width, width)
    return mat, col


def gather_kernel(owners_hbm, grad_hbm, out_ref, owners_ref, slot_of, grad, owners_sem, sems):
    mats, rows, cols = grad_hbm.shape
    slots = out_ref.shape[0]
    width = out_ref.shape[2] - LANES
    col_blocks = cols // width
    blocks = mats * col_blocks
    pieces = sems.shape[0]
    step = mats // pieces

    owners = pltpu.make_async_copy(owners_hbm, owners_ref, owners_sem)
    owners.start()
    loads = []
    for k in range(pieces):
        part = pl.ds(k * step, step)
        loads.append(pltpu.make_async_copy(grad_hbm.at[part], grad.at[part], sems.at[k]))
        loads[-1].start()

    owners.wait()

    def invert(s, spare):
        owner = owners_ref[s]
        slot_of[owner] = s
        shifted = (s,) + spare[:-1]
        return tuple(jnp.where(owner >= blocks, new, old) for new, old in zip(shifted, spare))

    spare = lax.fori_loop(0, slots, invert, (jnp.int32(0),) * (slots - blocks), unroll=16)
    for s in spare:
        out_ref[s, :, :width] = jnp.zeros((rows, width), jnp.bfloat16)

    def send(i, acc):
        for c in range(col_blocks):
            x = grad[i, :, c * width : (c + 1) * width]
            out_ref[slot_of[i * col_blocks + c], :, :width] = x
            x = x.astype(jnp.float32)
            x = x * x
            parts = [x[:, k * LANES : (k + 1) * LANES] for k in range(width // LANES)]
            while len(parts) > 1:
                parts = [p + q for p, q in zip(parts[::2], parts[1::2])]
            acc = acc + parts[0]
        return acc

    acc = jnp.zeros((rows, LANES), jnp.float32)
    for k in range(pieces):
        loads[k].wait()
        acc = lax.fori_loop(k * step, (k + 1) * step, send, acc)

    total = jnp.broadcast_to(jnp.sum(acc, axis=0, keepdims=True), (rows, LANES))
    high = total.astype(jnp.bfloat16).astype(jnp.float32)
    rest = jnp.where(high == jnp.inf, 0.0, total - high)
    middle = rest.astype(jnp.bfloat16).astype(jnp.float32)
    low = rest - middle
    row = lax.broadcasted_iota(jnp.int32, (rows, LANES), 0)
    note = jnp.where(row == 0, high, jnp.where(row == 1, middle, jnp.where(row == 2, low, 0.0)))
    out_ref[:, :, width:] = jnp.broadcast_to(note.astype(jnp.bfloat16)[None], (slots, rows, LANES))


def gather(owners, gradient, slots, width):
    mats, rows, _ = gradient.shape
    pieces = 5 if mats % 5 == 0 else 1
    table = pltpu.SMEM((slots,), jnp.int32)
    return pl.pallas_call(
        gather_kernel,
        out_shape=pltpu.VMEM((slots, rows, width + LANES), jnp.bfloat16),
        in_specs=[pl.BlockSpec(memory_space=pltpu.HBM)] * 2,
        out_specs=pl.BlockSpec(memory_space=pltpu.VMEM),
        scratch_shapes=[
            table,
            table,
            pltpu.VMEM(gradient.shape, jnp.bfloat16),
            pltpu.SemaphoreType.DMA,
            pltpu.SemaphoreType.DMA((pieces,)),
        ],
        compiler_params=pltpu.CompilerParams(vmem_limit_bytes=16 * MIB),
        cost_estimate=pl.CostEstimate(flops=10**11, bytes_accessed=10**8, transcendentals=0),
        name="gather_blocks",
    )(owners, gradient)


def place_kernel(owners_ref, rows_ref, out_ref, sem):
    slots, _, width = rows_ref.shape
    mats, _, cols = out_ref.shape
    col_blocks = cols // width
    blocks = mats * col_blocks

    def put(s, carry):
        owner = owners_ref[s]

        @pl.when(owner < blocks)
        def _():
            mat, col = block_place(owner, col_blocks, width)
            pltpu.make_async_copy(rows_ref.at[s], out_ref.at[mat, :, pl.ds(col, width)], sem).start()

        return carry

    lax.fori_loop(0, slots, put, 0, unroll=8)
    pltpu.make_async_copy(out_ref, out_ref, sem).wait()


def place(owners, rows, out_shape):
    return pl.pallas_call(
        place_kernel,
        out_shape=jax.ShapeDtypeStruct(out_shape, jnp.bfloat16),
        in_specs=[pl.BlockSpec(memory_space=pltpu.SMEM), pl.BlockSpec(memory_space=pltpu.VMEM)],
        out_specs=pl.BlockSpec(memory_space=pltpu.HBM),
        scratch_shapes=[pltpu.SemaphoreType.DMA],
        compiler_params=pltpu.CompilerParams(vmem_limit_bytes=16 * MIB),
        name="place_blocks",
    )(owners, rows)


def dot(a, b):
    return jnp.dot(a, b, preferred_element_type=jnp.float32)


def step_kernel(
    elements, g, r, l, m, s, u, nm_hbm, ns_hbm,
    lt, half, ratio, back, nm, ns, nm_sems, ns_sems,
):
    size = lt.shape[0]
    tiles = size // TILE

    def cols(j):
        return pl.ds(j * TILE, TILE)

    def tile_out(src, dst, sems, j):
        return pltpu.make_async_copy(src.at[:, cols(j)], dst.at[0, :, cols(j)], sems.at[j])

    total_sq = jnp.sum(g[:, size:].astype(jnp.float32), axis=(0, 1), keepdims=True)
    clip_factor = jnp.minimum(1.0, clip_rms * lax.rsqrt(total_sq / elements + 1e-06))
    correction = 1.0 - decay_rate**STEP

    for j in range(tiles):
        lt[:, cols(j)] = l[0, cols(j), :].T
    for j in range(tiles):
        half[:, cols(j)] = dot(g[:, :size], r[0, :, cols(j)]).astype(jnp.bfloat16)
    for j in range(tiles):
        rotated = clip_factor * dot(lt[...], half[:, cols(j)])
        scaled = (1.0 - decay_rate) * rotated
        first_mean = decay_rate * m[0, :, cols(j)].astype(jnp.float32) + scaled
        new_second = decay_rate * s[0, :, cols(j)] + scaled * rotated
        nm[:, cols(j)] = first_mean.astype(jnp.bfloat16)
        ns[:, cols(j)] = new_second
        root = new_second * lax.rsqrt(new_second)
        denominator = root + epsilon_adam * correction**0.5
        ratio[:, cols(j)] = (first_mean * correction**-0.5 / denominator).astype(jnp.bfloat16)
    for j in range(tiles):
        tile_out(nm, nm_hbm, nm_sems, j).start()
        tile_out(ns, ns_hbm, ns_sems, j).start()
    for j in range(tiles):
        back[:, cols(j)] = dot(l[0], ratio[:, cols(j)]).astype(jnp.bfloat16)
    for j in range(tiles):
        u[:, cols(j)] = lax.dot_general(
            back[...], r[0, cols(j), :], (((1,), (1,)), ((), ())), preferred_element_type=jnp.float32
        ).astype(jnp.bfloat16)
    for j in range(tiles):
        tile_out(nm, nm_hbm, nm_sems, j).wait()
        tile_out(ns, ns_hbm, ns_sems, j).wait()


def slot_step(elements, g, right, left, moment, second):
    size = g.shape[0]
    tiles = size // TILE
    low = pltpu.VMEM((size, size), jnp.bfloat16)
    wide = pltpu.VMEM((size, size), jnp.float32)
    vmem = pl.BlockSpec(memory_space=pltpu.VMEM)
    hbm = pl.BlockSpec(memory_space=pltpu.HBM)

    def kernel(*refs):
        step_kernel(elements, *refs)

    return pl.pallas_call(
        kernel,
        out_shape=(
            pltpu.VMEM((size, size), jnp.bfloat16),
            jax.ShapeDtypeStruct((1, size, size), jnp.bfloat16),
            jax.ShapeDtypeStruct((1, size, size), jnp.float32),
        ),
        in_specs=[vmem] * 5,
        out_specs=(vmem, hbm, hbm),
        scratch_shapes=[low, low, low, low, low, wide]
        + [pltpu.SemaphoreType.DMA((tiles,))] * 2,
        compiler_params=pltpu.CompilerParams(vmem_limit_bytes=36 * MIB),
        cost_estimate=pl.CostEstimate(flops=8 * size**3, bytes_accessed=24 * size**2, transcendentals=2 * size**2),
        name="slot_step",
    )(g, right, left, moment, second)


def exchange(x):
    return lax.all_to_all(x, AXES, split_axis=0, concat_axis=0, tiled=True)


def shards(gradient, left_basis, right_basis, moment, second, owners):
    group_size = lax.axis_size(AXES)
    matrices, row_count, col_count = gradient.shape
    block_size = left_basis.shape[1]
    element_count = matrices * row_count * col_count * group_size
    gradient = pltpu.with_memory_space_constraint(gradient, pltpu.HBM)

    sending = gather(pltpu.with_memory_space_constraint(owners, pltpu.HBM), gradient, group_size, block_size)
    arrived = exchange(sending)
    update, new_moment, new_second = slot_step(
        element_count, arrived.reshape(block_size, block_size + LANES),
        right_basis, left_basis, moment, second,
    )
    returned = exchange(update.reshape(group_size, row_count, block_size))
    direction = place(owners, returned, gradient.shape)
    return (direction, new_moment, new_second)


def solution(mesh):
    return jax.shard_map(
        shards,
        mesh=mesh,
        in_specs=(
            P(None, AXES, None),
            P(AXES, None, None),
            P(AXES, None, None),
            P(AXES, None, None),
            P(AXES, None, None),
            P(),
        ),
        out_specs=(
            P(None, AXES, None),
            P(AXES, None, None),
            P(AXES, None, None),
        ),
        check_vma=False,
    )
```

```python
import jax
import jax.numpy as jnp
from jax import lax
from jax.experimental import pallas as pl
from jax.experimental.pallas import tpu as pltpu
from jax.sharding import PartitionSpec as P

STEP = 10

decay_rate = 0.95
clip_rms = 0.5
epsilon_adam = 1e-08

AXES = ("rep", "fsdp")
TILE = 1024
LANES = 128
MIB = 1024 * 1024


def block_place(block, col_blocks, width):
    mat = (block * (1024 // col_blocks + 1)) >> 10
    col = pl.multiple_of((block - mat * col_blocks) * width, width)
    return mat, col


def gather_kernel(owners_hbm, grad_hbm, out_ref, owners_ref, slot_of, grad, owners_sem, sems):
    mats, rows, cols = grad_hbm.shape
    slots = out_ref.shape[0]
    width = out_ref.shape[2] - LANES
    col_blocks = cols // width
    blocks = mats * col_blocks
    pieces = sems.shape[0]
    step = mats // pieces

    owners = pltpu.make_async_copy(owners_hbm, owners_ref, owners_sem)
    owners.start()
    loads = []
    for k in range(pieces):
        part = pl.ds(k * step, step)
        loads.append(pltpu.make_async_copy(grad_hbm.at[part], grad.at[part], sems.at[k]))
        loads[-1].start()

    owners.wait()

    def invert(s, spare):
        owner = owners_ref[s]
        slot_of[owner] = s
        shifted = (s,) + spare[:-1]
        return tuple(jnp.where(owner >= blocks, new, old) for new, old in zip(shifted, spare))

    spare = lax.fori_loop(0, slots, invert, (jnp.int32(0),) * (slots - blocks), unroll=16)
    for s in spare:
        out_ref[s, :, :width] = jnp.zeros((rows, width), jnp.bfloat16)

    def send(i, acc):
        for c in range(col_blocks):
            x = grad[i, :, c * width : (c + 1) * width]
            out_ref[slot_of[i * col_blocks + c], :, :width] = x
            x = x.astype(jnp.float32)
            x = x * x
            parts = [x[:, k * LANES : (k + 1) * LANES] for k in range(width // LANES)]
            while len(parts) > 1:
                parts = [p + q for p, q in zip(parts[::2], parts[1::2])]
            acc = acc + parts[0]
        return acc

    acc = jnp.zeros((rows, LANES), jnp.float32)
    for k in range(pieces):
        loads[k].wait()
        acc = lax.fori_loop(k * step, (k + 1) * step, send, acc)

    total = jnp.broadcast_to(jnp.sum(acc, axis=0, keepdims=True), (rows, LANES))
    high = total.astype(jnp.bfloat16).astype(jnp.float32)
    rest = jnp.where(high == jnp.inf, 0.0, total - high)
    middle = rest.astype(jnp.bfloat16).astype(jnp.float32)
    low = rest - middle
    row = lax.broadcasted_iota(jnp.int32, (rows, LANES), 0)
    note = jnp.where(row == 0, high, jnp.where(row == 1, middle, jnp.where(row == 2, low, 0.0)))
    out_ref[:, :, width:] = jnp.broadcast_to(note.astype(jnp.bfloat16)[None], (slots, rows, LANES))


def gather(owners, gradient, slots, width):
    mats, rows, _ = gradient.shape
    pieces = 5 if mats % 5 == 0 else 1
    table = pltpu.SMEM((slots,), jnp.int32)
    return pl.pallas_call(
        gather_kernel,
        out_shape=pltpu.VMEM((slots, rows, width + LANES), jnp.bfloat16),
        in_specs=[pl.BlockSpec(memory_space=pltpu.HBM)] * 2,
        out_specs=pl.BlockSpec(memory_space=pltpu.VMEM),
        scratch_shapes=[
            table,
            table,
            pltpu.VMEM(gradient.shape, jnp.bfloat16),
            pltpu.SemaphoreType.DMA,
            pltpu.SemaphoreType.DMA((pieces,)),
        ],
        compiler_params=pltpu.CompilerParams(vmem_limit_bytes=16 * MIB),
        cost_estimate=pl.CostEstimate(flops=10**11, bytes_accessed=10**8, transcendentals=0),
        name="gather_blocks",
    )(owners, gradient)


def place_kernel(owners_ref, rows_ref, out_ref, sem):
    slots, _, width = rows_ref.shape
    mats, _, cols = out_ref.shape
    col_blocks = cols // width
    blocks = mats * col_blocks

    def put(s, carry):
        owner = owners_ref[s]

        @pl.when(owner < blocks)
        def _():
            mat, col = block_place(owner, col_blocks, width)
            pltpu.make_async_copy(rows_ref.at[s], out_ref.at[mat, :, pl.ds(col, width)], sem).start()

        return carry

    lax.fori_loop(0, slots, put, 0, unroll=8)
    pltpu.make_async_copy(out_ref, out_ref, sem).wait()


def place(owners, rows, out_shape):
    return pl.pallas_call(
        place_kernel,
        out_shape=jax.ShapeDtypeStruct(out_shape, jnp.bfloat16),
        in_specs=[pl.BlockSpec(memory_space=pltpu.SMEM), pl.BlockSpec(memory_space=pltpu.VMEM)],
        out_specs=pl.BlockSpec(memory_space=pltpu.HBM),
        scratch_shapes=[pltpu.SemaphoreType.DMA],
        compiler_params=pltpu.CompilerParams(vmem_limit_bytes=16 * MIB),
        name="place_blocks",
    )(owners, rows)


def dot(a, b):
    return jnp.dot(a, b, preferred_element_type=jnp.float32)


def step_kernel(
    elements, g, r, l, m, s, u, nm_hbm, ns_hbm,
    lt, half, ratio, back, nm, ns, nm_sems, ns_sems,
):
    size = lt.shape[0]
    tiles = size // TILE

    def cols(j):
        return pl.ds(j * TILE, TILE)

    def tile_out(src, dst, sems, j):
        return pltpu.make_async_copy(src.at[:, cols(j)], dst.at[0, :, cols(j)], sems.at[j])

    total_sq = jnp.sum(g[:, size:].astype(jnp.float32), axis=(0, 1), keepdims=True)
    clip_factor = jnp.minimum(1.0, clip_rms * lax.rsqrt(total_sq / elements + 1e-06))
    correction = 1.0 - decay_rate**STEP

    for j in range(tiles):
        lt[:, cols(j)] = l[0, cols(j), :].T
    for j in range(tiles):
        half[:, cols(j)] = dot(g[:, :size], r[0, :, cols(j)]).astype(jnp.bfloat16)
    for j in range(tiles):
        rotated = clip_factor * dot(lt[...], half[:, cols(j)])
        scaled = (1.0 - decay_rate) * rotated
        first_mean = decay_rate * m[0, :, cols(j)].astype(jnp.float32) + scaled
        new_second = decay_rate * s[0, :, cols(j)] + scaled * rotated
        nm[:, cols(j)] = first_mean.astype(jnp.bfloat16)
        ns[:, cols(j)] = new_second
        root = new_second * lax.rsqrt(new_second)
        denominator = root + epsilon_adam * correction**0.5
        ratio[:, cols(j)] = (first_mean * correction**-0.5 / denominator).astype(jnp.bfloat16)
    for j in range(tiles):
        tile_out(nm, nm_hbm, nm_sems, j).start()
        tile_out(ns, ns_hbm, ns_sems, j).start()
    for j in range(tiles):
        back[:, cols(j)] = dot(l[0], ratio[:, cols(j)]).astype(jnp.bfloat16)
    for j in range(tiles):
        u[:, cols(j)] = lax.dot_general(
            back[...], r[0, cols(j), :], (((1,), (1,)), ((), ())), preferred_element_type=jnp.float32
        ).astype(jnp.bfloat16)
    for j in range(tiles):
        tile_out(nm, nm_hbm, nm_sems, j).wait()
        tile_out(ns, ns_hbm, ns_sems, j).wait()


def slot_step(elements, g, right, left, moment, second):
    size = g.shape[0]
    tiles = size // TILE
    low = pltpu.VMEM((size, size), jnp.bfloat16)
    wide = pltpu.VMEM((size, size), jnp.float32)
    vmem = pl.BlockSpec(memory_space=pltpu.VMEM)
    hbm = pl.BlockSpec(memory_space=pltpu.HBM)

    def kernel(*refs):
        step_kernel(elements, *refs)

    return pl.pallas_call(
        kernel,
        out_shape=(
            pltpu.VMEM((size, size), jnp.bfloat16),
            jax.ShapeDtypeStruct((1, size, size), jnp.bfloat16),
            jax.ShapeDtypeStruct((1, size, size), jnp.float32),
        ),
        in_specs=[vmem] * 5,
        out_specs=(vmem, hbm, hbm),
        scratch_shapes=[low, low, low, low, low, wide]
        + [pltpu.SemaphoreType.DMA((tiles,))] * 2,
        compiler_params=pltpu.CompilerParams(vmem_limit_bytes=36 * MIB),
        cost_estimate=pl.CostEstimate(flops=8 * size**3, bytes_accessed=24 * size**2, transcendentals=2 * size**2),
        name="slot_step",
    )(g, right, left, moment, second)


def exchange(x):
    return lax.all_to_all(x, AXES, split_axis=0, concat_axis=0, tiled=True)


def shards(gradient, left_basis, right_basis, moment, second, owners):
    group_size = lax.axis_size(AXES)
    matrices, row_count, col_count = gradient.shape
    block_size = left_basis.shape[1]
    element_count = matrices * row_count * col_count * group_size
    gradient = pltpu.with_memory_space_constraint(gradient, pltpu.HBM)

    sending = gather(pltpu.with_memory_space_constraint(owners, pltpu.HBM), gradient, group_size, block_size)
    arrived = exchange(sending)
    update, new_moment, new_second = slot_step(
        element_count, arrived.reshape(block_size, block_size + LANES),
        right_basis, left_basis, moment, second,
    )
    returned = exchange(update.reshape(group_size, row_count, block_size))
    direction = place(owners, returned, gradient.shape)
    return (direction, new_moment, new_second)


def solution(mesh):
    return jax.shard_map(
        shards,
        mesh=mesh,
        in_specs=(
            P(None, AXES, None),
            P(AXES, None, None),
            P(AXES, None, None),
            P(AXES, None, None),
            P(AXES, None, None),
            P(),
        ),
        out_specs=(
            P(None, AXES, None),
            P(AXES, None, None),
            P(AXES, None, None),
        ),
        check_vma=False,
    )
```
